32 devices in a mesh: ka: 16 (over z, y, core), rad: 2 (over x).
Axes of the slice: x: 2, y: 2, z: 4, core: 2. Of those that a mesh axis runs over, the one named last changes fastest.
Arguments:
- prev_wave: float32 [16, 192, 16, 128], P('ka', None, 'rad'), may hold values from -6 to 6
- cur_wave: float32 [16, 192, 16, 128], P('ka', None, 'rad'), may hold values from -6 to 6
- legendre: float32 [16, 192, 192], P('ka'), may hold values from -0.4375 to 0.4375
- potential: float32 [192, 16, 128], P(None, 'rad'), may hold values from -0.15 to 0.15
- radial: float32 [3, 16], P(None, 'rad'), may hold values from 0.02 to 0.3
- rot_const: float32 [128], replicated, may hold values from 0.05 to 0.5
- first_row: int32 [16], P('ka'), may hold values from 0 to 96, as said below
Outputs:
- prev_out: float32 [16, 192, 16, 128], P('ka', None, 'rad')
- cur_out: float32 [16, 192, 16, 128], P('ka', None, 'rad')
The draws below stay inside these ranges and needn't reach their ends.
Inputs may be any that keep to these rules, and one draw needn't show every extreme that they name: first_row never falls with K, first_row[0] = 0 and first_row[15] = 96.
All inputs are finite; a program needn't handle non-finite values.
Results may differ from the reference program's by a relative error of at most 0.0003.
Values sent between devices are 32-bit elements; how exact they have to be, the bound alone decides.
A program may use at most 64 MiB of HBM per device.

```python
import math
import jax
import jax.numpy as jnp
from jax import lax

NJ = 192
NRR = 128
STEPS = 4
KICKS = 2
NR = 16
KTOT = 16
LMAX = 96


def draw_first_row(key, part):
    inner = jax.random.randint(jax.random.fold_in(key, 17), (KTOT - 2,), 0, LMAX + 1)
    inner = jnp.sort(inner)
    start = jnp.zeros((1,), jnp.int32)
    finish = jnp.full((1,), LMAX, jnp.int32)
    return jnp.concatenate([start, inner.astype(jnp.int32), finish]).astype(jnp.int32)


def steps_of(stream_key, shape, pieces, smallest, largest):
    factor_of, own = 1.0, jax.random.fold_in(stream_key, 6)
    for axis_at, shards_of in pieces:
        draws = jnp.exp(jax.random.uniform(jax.random.fold_in(own, axis_at), (shards_of,), jnp.float32, smallest / len(pieces), largest / len(pieces)))
        factor_of = factor_of * jnp.repeat(draws, shape[axis_at] // shards_of).reshape([-1 if axis == axis_at else 1 for axis in range(len(shape))])
    return factor_of


def normal_values(own_key, extent, deviation, most, shards=(), held_as=jnp.bfloat16):
    entries = jax.random.normal(own_key, extent, jnp.float32) * deviation
    if len(shards) > 0:
        entries = steps_of(own_key, extent, shards, -0.22, 0.18) * entries
    return jnp.clip(entries, min=-most, max=most).astype(held_as)


def setup_inputs(seed: int = 0) -> dict:
    arg_keys = jax.random.split(jax.random.key(seed), 8)
    prev_wave = normal_values(arg_keys[0], (KTOT, NJ, NR, NRR), 1.0, 6.0, ((0, 16), (2, 2)), jnp.float32)
    cur_wave = normal_values(arg_keys[1], (KTOT, NJ, NR, NRR), 1.0, 6.0, ((0, 16), (2, 2)), jnp.float32)
    legendre = normal_values(arg_keys[2], (KTOT, NJ, NJ), NJ ** -0.5, 0.4375, ((0, 16),), jnp.float32)
    potential = jnp.clip(jax.random.uniform(arg_keys[3], (NJ, NR, NRR), jnp.float32, -0.15, 0.15) * steps_of(arg_keys[3], (NJ, NR, NRR), ((1, 2),), -0.4, 0.0), -0.15, 0.15)
    radial = jnp.clip(jnp.exp(math.log(0.3) - 2.7080503 * jax.random.uniform(arg_keys[4], (3, NR), jnp.float32) ** steps_of(arg_keys[4], (3, NR), ((1, 2),), -0.2, 0.2)), 0.02, 0.3)
    rot_const = jnp.clip(jnp.exp(jax.random.uniform(arg_keys[5], (NRR,), jnp.float32, math.log(0.05), math.log(0.5))), 0.05, 0.5)
    first_row = draw_first_row(jax.random.fold_in(arg_keys[7], 71), 0)
    return {"prev_wave": prev_wave, "cur_wave": cur_wave, "legendre": legendre, "potential": potential, "radial": radial, "rot_const": rot_const, "first_row": first_row}


COEF = 0.1
RKIN = 0.04
EMID = 0.75

def sinc_table(count):
    index = jnp.arange(count, dtype=jnp.int32)
    differ = index[:, None] - index[None, :]
    parity = (1 - 2 * (jnp.abs(differ) % 2)).astype(jnp.float32)
    square = jnp.maximum(differ * differ, 1).astype(jnp.float32)
    table = jnp.where(differ == 0, jnp.float32(math.pi * math.pi / 3.0), 2.0 * parity / square)
    return (RKIN * table).astype(jnp.float32)

def coupling(jidx, kval, jtop, nrot):
    first = jnp.maximum(jidx * (jidx + 1) - kval * (kval + 1), 0)
    second = jnp.maximum(jtop * (jtop + 1) - kval * (kval + 1), 0)
    return jnp.sqrt((first * second).astype(jnp.float32)) / (nrot * (jtop + 1))

def reference(prev_wave, cur_wave, legendre, potential, radial, rot_const, first_row):
    jtop = KTOT - 1
    jidx = jnp.arange(NJ, dtype=jnp.int32)
    kidx = jnp.arange(KTOT, dtype=jnp.int32)
    live = (jidx[None, :] >= first_row[:, None]).astype(jnp.float32)[:, :, None, None]
    qrot = (jidx * (jidx + 1)).astype(jnp.float32) / (NJ * (NJ + 1))
    pkay = (jtop * (jtop + 1) - 2 * kidx * kidx).astype(jnp.float32) / (NJ * (NJ + 1))
    damp = jnp.exp(-radial[2])[None, None, :, None]
    corio = radial[1][None, None, :, None]
    couple = coupling(jidx[None, :], kidx[:, None], jtop, NJ)
    couple_low = jnp.concatenate([jnp.zeros((1, NJ), jnp.float32), couple[:-1]], axis=0)
    table = sinc_table(NRR)
    diag = rot_const[None, None, None, :] * qrot[None, :, None, None] + radial[0][None, None, :, None] * (qrot[None, :, None, None] + pkay[:, None, None, None]) - EMID

    def apply_h(wave):
        zero = jnp.zeros_like(wave[:1])
        upper = jnp.concatenate([wave[1:], zero], axis=0)
        lower = jnp.concatenate([zero, wave[:-1]], axis=0)
        coriolis = corio * (couple[:, :, None, None] * upper + couple_low[:, :, None, None] * lower)
        padded = jnp.pad(wave, ((0, 0), (0, 0), (1, 1), (0, 0)))
        stencil = 2.0 * wave - padded[:, :, 2:] - padded[:, :, :-2]
        kinetic = jnp.einsum('kjRr,rs->kjRs', wave, table, precision=lax.Precision.HIGHEST)
        angular = jnp.einsum('kjt,kjRr->ktRr', legendre, wave, precision=lax.Precision.HIGHEST)
        back = jnp.einsum('kjt,ktRr->kjRr', legendre, potential[None] * angular, precision=lax.Precision.HIGHEST)
        return live * (COEF * stencil + kinetic + diag * wave + back + coriolis)
    prev = live * prev_wave
    cur = live * cur_wave
    for kick_turn in range(KICKS):
        for step in range(STEPS):
            newer = damp * (2.0 * apply_h(cur) - damp * prev)
            prev, cur = (cur, newer)
    return (prev, cur)
```

```python
import functools
import math

import jax
import jax.numpy as jnp
from jax import lax
from jax.experimental import pallas as pl
from jax.experimental.pallas import tpu as pltpu
from jax.sharding import PartitionSpec as P

STEPS = 4
KICKS = 2
COEF = 0.1
RKIN = 0.04
EMID = 0.75
MESH = pl.DeviceIdType.MESH


def sinc_table(count):
    index = jnp.arange(count, dtype=jnp.int32)
    differ = index[:, None] - index[None, :]
    parity = (1 - 2 * (jnp.abs(differ) % 2)).astype(jnp.float32)
    square = jnp.maximum(differ * differ, 1).astype(jnp.float32)
    table = jnp.where(differ == 0, jnp.float32(math.pi * math.pi / 3.0), 2.0 * parity / square)
    return RKIN * table


def coupling(jidx, kval, jtop, nrot):
    first = jnp.maximum(jidx * (jidx + 1) - kval * (kval + 1), 0)
    second = jnp.maximum(jtop * (jtop + 1) - kval * (kval + 1), 0)
    return jnp.sqrt((first * second).astype(jnp.float32)) / (nrot * (jtop + 1))


def halves(x):
    top = lax.reduce_precision(x, 8, 7)
    return top.astype(jnp.bfloat16), (x - top).astype(jnp.bfloat16)


def split(x):
    top = x.astype(jnp.bfloat16)
    return top, (x - top.astype(jnp.float32)).astype(jnp.bfloat16)


def kernel(
    nka, nrad, steps, rc,
    cur_ref, prev_ref, la_ref, lb_ref, table_ref, pot_ref, diag_ref, shi_ref, slo_ref, scal_ref,
    wave,
    from_lo, from_hi, from_prev, from_next,
    k_send, k_recv, r_send, r_recv,
):
    ka, rad = lax.axis_index("ka"), lax.axis_index("rad")
    m = ka % 4
    y, c = m // 2, m % 2
    pair = (ka // 4) * 2 + c
    flip = (y + rad) % 2
    chunk = 2 * rad + flip
    has = {
        "lo": pair > 0,
        "hi": pair < nka // 2 - 1,
        "prev": chunk > 0,
        "next": chunk < 2 * nrad - 1,
    }
    other = ka + 2 - 4 * y
    dev = {
        "lo": (jnp.maximum(jnp.where(c == 1, ka - 1, ka - 3), 0), rad),
        "hi": (jnp.minimum(jnp.where(c == 0, ka + 1, ka + 3), nka - 1), rad),
        "prev": (jnp.where(flip == 1, other, ka), jnp.where(flip == 1, rad, jnp.maximum(rad - 1, 0))),
        "next": (jnp.where(flip == 0, other, ka), jnp.where(flip == 0, rad, jnp.minimum(rad + 1, nrad - 1))),
    }
    lands = {"lo": from_hi, "hi": from_lo, "prev": from_next, "next": from_prev}
    lane = {"lo": 0, "hi": 1, "prev": 0, "next": 1}

    def copy(side, slot, k, r):
        if side in ("lo", "hi"):
            sems, at = (k_send, k_recv), r
        else:
            sems, at = (r_send, r_recv), k
        return pltpu.make_async_remote_copy(
            src_ref=wave.at[slot, k, r],
            dst_ref=lands[side].at[slot, at],
            send_sem=sems[0].at[slot, lane[side], at],
            recv_sem=sems[1].at[slot, lane[side], at],
            device_id=dev[side],
            device_id_type=MESH,
        )

    def sides_of(k, r):
        found = ["lo" if k == 0 else "hi"]
        if r == 0:
            found.append("prev")
        if r == rc - 1:
            found.append("next")
        return found

    def send(slot, k, r):
        for side in sides_of(k, r):
            @pl.when(has[side])
            def _():
                copy(side, slot, k, r).start()

    opposite = {"lo": "hi", "hi": "lo", "prev": "next", "next": "prev"}

    def receive(slot, k, r):
        for side in sides_of(k, r):
            @pl.when(has[side])
            def _():
                copy(opposite[side], slot, k, r).wait_recv()

    order = []
    for i in range(rc // 2):
        order.append((i, rc - 1 - i))

    for side, buf in (("lo", from_lo), ("hi", from_hi), ("prev", from_prev), ("next", from_next)):
        @pl.when(jnp.logical_not(has[side]))
        def _():
            buf[...] = jnp.zeros_like(buf)

    wave[0] = cur_ref[...]
    barrier = pltpu.get_barrier_semaphore()
    for side in dev:
        @pl.when(has[side])
        def _():
            pl.semaphore_signal(barrier, inc=1, device_id=dev[side], device_id_type=MESH)
    pl.semaphore_wait(barrier, sum(has[side].astype(jnp.int32) for side in dev))
    for rs in order:
        for r in rs:
            for k in range(2):
                send(0, k, r)
    wave[1] = prev_ref[...]

    def step(n, last):
        s = lax.rem(n, 2)
        t = 1 - s
        for i, rs in enumerate(order):
            for k in range(2):
                both = jnp.concatenate([wave[s, k, rs[0]], wave[s, k, rs[1]]], axis=1)
                top, low = split(both)
                ang = jnp.dot(
                    la_ref[k], jnp.concatenate([top, top, low], axis=0),
                    preferred_element_type=jnp.float32,
                )
                ptop, plow = split(ang * pot_ref[i])
                back = jnp.dot(
                    lb_ref[k], jnp.concatenate([ptop, ptop, plow], axis=0),
                    preferred_element_type=jnp.float32,
                )
                width = both.shape[1] // 2
                for e, r in enumerate(rs):
                    cols = slice(e * width, (e + 1) * width)
                    kin = jnp.dot(
                        jnp.concatenate([top[:, cols], low[:, cols]], axis=1), table_ref[...],
                        preferred_element_type=jnp.float32,
                    )
                    kin = kin[:, :width] + kin[:, width:]
                    wave[t, k, r] = (
                        diag_ref[k, r] * wave[s, k, r]
                        + scal_ref[0, r] * kin
                        + back[:, cols]
                        - scal_ref[1, r] * wave[t, k, r]
                    )
            for r in rs:
                for k in range(2):
                    receive(s, k, r)
                    ahead = wave[s, k, r + 1] if r < rc - 1 else from_next[s, k]
                    behind = wave[s, k, r - 1] if r > 0 else from_prev[s, k]
                    upper = wave[s, 1, r] if k == 0 else from_hi[s, r]
                    lower = from_lo[s, r] if k == 0 else wave[s, 0, r]
                    wave[t, k, r] = (
                        wave[t, k, r]
                        - scal_ref[2, r] * (ahead + behind)
                        + scal_ref[3, r] * (shi_ref[k] * upper + slo_ref[k] * lower)
                    )
                    if not last:
                        send(t, k, r)
        for rs in order:
            for r in rs:
                for k in range(2):
                    for side in sides_of(k, r):
                        @pl.when(has[side])
                        def _():
                            copy(side, s, k, r).wait_send()

    def body(n, carry):
        step(n, False)
        return carry

    lax.fori_loop(0, steps - 1, body, 0)
    step(steps - 1, True)


def on_device(prev_wave, cur_wave, legendre, potential, radial, rot_const, first_row):
    nka, nrad = lax.axis_size("ka"), lax.axis_size("rad")
    ka, rad = lax.axis_index("ka"), lax.axis_index("rad")
    nrot, rows, width = cur_wave.shape[1:]
    rc = rows // 2
    m = ka % 4
    hi_bit, lo_bit = m // 2, m % 2
    group = ka // 4
    odd = rad % 2
    jtop = nka - 1
    jidx = jnp.arange(nrot, dtype=jnp.int32)
    swap_a, swap_b = [], []
    for i in range(nka):
        c, b = (i % 4) // 2, i % 2
        swap_a.append((i, i - i % 4 + 2 * b + c))
        swap_b.append((i, i - i % 4 + 2 * (1 - b) + c))
    inverse_a = [(j, i) for i, j in swap_a]
    inverse_b = [(j, i) for i, j in swap_b]

    mine = (jidx >= first_row[0]).astype(jnp.float32)

    def spread(wave):
        moved = jnp.transpose(wave[0] * mine[:, None, None], (1, 0, 2))
        first = lax.dynamic_slice_in_dim(moved, (lo_bit ^ odd) * rc, rc, 0)
        second = lax.dynamic_slice_in_dim(moved, (1 - (lo_bit ^ odd)) * rc, rc, 0)
        a = lax.ppermute(first, "ka", swap_a)
        b = lax.ppermute(second, "ka", swap_b)
        return jnp.where(hi_bit == 0, jnp.stack([a, b]), jnp.stack([b, a]))

    def unspread(waves):
        a = lax.ppermute(jnp.where(hi_bit == 0, waves[0], waves[1]), "ka", inverse_a)
        b = lax.ppermute(jnp.where(hi_bit == 0, waves[1], waves[0]), "ka", inverse_b)
        whole = jnp.where((lo_bit ^ odd) == 0, jnp.concatenate([a, b]), jnp.concatenate([b, a]))
        return jnp.transpose(whole, (1, 0, 2))[None]

    packed = jnp.concatenate(
        [legendre[0] * mine[:, None], jnp.broadcast_to(first_row[0].astype(jnp.float32), (8, nrot))]
    )
    cur = spread(cur_wave)
    pa = lax.ppermute(packed, "ka", swap_a)
    pb = lax.ppermute(packed, "ka", swap_b)
    prev = spread(prev_wave)
    both = jnp.where(hi_bit == 0, jnp.stack([pa, pb]), jnp.stack([pb, pa]))
    leg = both[:, :nrot]
    firsts = both[:, nrot, 0]
    live = (jidx.astype(jnp.float32)[None, :] >= firsts[:, None]).astype(jnp.float32)

    half = hi_bit ^ odd
    local = lax.dynamic_slice_in_dim(radial, half * rc, rc, 1)
    damp = jnp.exp(-local[2])
    scal = jnp.stack([damp, damp * damp, 2.0 * COEF * damp, 2.0 * local[1] * damp])
    kval = 4 * group + 2 * lo_bit + jnp.arange(2, dtype=jnp.int32)
    qrot = (jidx * (jidx + 1)).astype(jnp.float32) / (nrot * (nrot + 1))
    pkay = (jtop * (jtop + 1) - 2 * kval * kval).astype(jnp.float32) / (nrot * (nrot + 1))
    diag = (
        rot_const[None, None, None, :] * qrot[None, None, :, None]
        + local[0][None, :, None, None] * (qrot[None, None, :, None] + pkay[:, None, None, None])
        - EMID
    )
    diag = 2.0 * damp[None, :, None, None] * (diag + 2.0 * COEF)
    s_here = live * coupling(jidx[None, :], kval[:, None], jtop, nrot)
    s_below = live * coupling(jidx[None, :], kval[:, None] - 1, jtop, nrot)
    s_here = jnp.broadcast_to(s_here[:, :, None], (2, nrot, width))
    s_below = jnp.broadcast_to(s_below[:, :, None], (2, nrot, width))

    top, low = halves(leg)
    lb = jnp.concatenate([top, low, top], axis=2)
    legt = jnp.transpose(leg, (0, 2, 1))
    top, low = halves(legt)
    la = jnp.concatenate([top, low, top], axis=2)
    top, low = halves(2.0 * sinc_table(width))
    row = jnp.concatenate([top, low], axis=1)
    table = jnp.concatenate([row, row], axis=0)
    pot = lax.dynamic_slice_in_dim(jnp.transpose(potential, (1, 0, 2)), half * rc, rc, 0)
    pot = pot * (2.0 * damp)[:, None, None]
    pot = jnp.stack([jnp.concatenate([pot[i], pot[rc - 1 - i]], axis=1) for i in range(rc // 2)])

    steps = STEPS * KICKS
    vmem = pl.BlockSpec(memory_space=pltpu.VMEM)
    point = (nrot, width)
    out = pl.pallas_call(
        functools.partial(kernel, nka, nrad, steps, rc),
        out_shape=jax.ShapeDtypeStruct((2, 2, rc) + point, jnp.float32),
        in_specs=[vmem] * 9 + [pl.BlockSpec(memory_space=pltpu.SMEM)],
        out_specs=vmem,
        scratch_shapes=[
            pltpu.VMEM((2, rc) + point, jnp.float32),
            pltpu.VMEM((2, rc) + point, jnp.float32),
            pltpu.VMEM((2, 2) + point, jnp.float32),
            pltpu.VMEM((2, 2) + point, jnp.float32),
            pltpu.SemaphoreType.DMA((2, 2, rc)),
            pltpu.SemaphoreType.DMA((2, 2, rc)),
            pltpu.SemaphoreType.DMA((2, 2, 2)),
            pltpu.SemaphoreType.DMA((2, 2, 2)),
        ],
        compiler_params=pltpu.CompilerParams(
            collective_id=0, has_side_effects=True, vmem_limit_bytes=40 * 1024 * 1024
        ),
    )(cur, prev, la, lb, table, pot, diag, s_here, s_below, scal)
    at = steps % 2
    return (unspread(out[1 - at]), unspread(out[at]))


def solution(mesh):
    placed = (
        P("ka", None, "rad", None),
        P("ka", None, "rad", None),
        P("ka", None, None),
        P(None, "rad", None),
        P(None, "rad"),
        P(),
        P("ka"),
    )
    return jax.shard_map(
        on_device,
        mesh=mesh,
        in_specs=placed,
        out_specs=(P("ka", None, "rad", None), P("ka", None, "rad", None)),
        check_vma=False,
    )
```

```python
import functools
import math

import jax
import jax.numpy as jnp
from jax import lax
from jax.experimental import pallas as pl
from jax.experimental.pallas import tpu as pltpu
from jax.sharding import PartitionSpec as P

STEPS = 4
KICKS = 2
COEF = 0.1
RKIN = 0.04
EMID = 0.75
MESH = pl.DeviceIdType.MESH


def sinc_table(count):
    index = jnp.arange(count, dtype=jnp.int32)
    differ = index[:, None] - index[None, :]
    parity = (1 - 2 * (jnp.abs(differ) % 2)).astype(jnp.float32)
    square = jnp.maximum(differ * differ, 1).astype(jnp.float32)
    table = jnp.where(differ == 0, jnp.float32(math.pi * math.pi / 3.0), 2.0 * parity / square)
    return RKIN * table


def coupling(jidx, kval, jtop, nrot):
    first = jnp.maximum(jidx * (jidx + 1) - kval * (kval + 1), 0)
    second = jnp.maximum(jtop * (jtop + 1) - kval * (kval + 1), 0)
    return jnp.sqrt((first * second).astype(jnp.float32)) / (nrot * (jtop + 1))


def halves(x):
    top = lax.reduce_precision(x, 8, 7)
    return top.astype(jnp.bfloat16), (x - top).astype(jnp.bfloat16)


def split(x):
    top = x.astype(jnp.bfloat16)
    return top, (x - top.astype(jnp.float32)).astype(jnp.bfloat16)


def kernel(
    nka, nrad, steps, rc,
    cur_ref, prev_ref, leg_ref, table_ref, pot_ref, diag_ref, here_ref, below_ref, scal_ref,
    prev_out, cur_out,
    wave, legs, la_ref, lb_ref, shi_ref, slo_ref,
    from_lo, from_hi, from_prev, from_next,
    k_send, k_recv, r_send, r_recv, in_send, in_recv, old_send, old_recv, new_send, new_recv,
):
    ka, rad = lax.axis_index("ka"), lax.axis_index("rad")
    m = ka % 4
    y, c = m // 2, m % 2
    pair = (ka // 4) * 2 + c
    flip = (y + rad) % 2
    chunk = 2 * rad + flip
    has = {
        "lo": pair > 0,
        "hi": pair < nka // 2 - 1,
        "prev": chunk > 0,
        "next": chunk < 2 * nrad - 1,
    }
    other = ka + 2 - 4 * y
    dev = {
        "lo": (jnp.maximum(jnp.where(c == 1, ka - 1, ka - 3), 0), rad),
        "hi": (jnp.minimum(jnp.where(c == 0, ka + 1, ka + 3), nka - 1), rad),
        "prev": (jnp.where(flip == 1, other, ka), jnp.where(flip == 1, rad, jnp.maximum(rad - 1, 0))),
        "next": (jnp.where(flip == 0, other, ka), jnp.where(flip == 0, rad, jnp.minimum(rad + 1, nrad - 1))),
    }
    lands = {"lo": from_hi, "hi": from_lo, "prev": from_next, "next": from_prev}
    lane = {"lo": 0, "hi": 1, "prev": 0, "next": 1}

    def copy(side, slot, k, r):
        if side in ("lo", "hi"):
            sems, at = (k_send, k_recv), r
        else:
            sems, at = (r_send, r_recv), k
        return pltpu.make_async_remote_copy(
            src_ref=wave.at[slot, k, r],
            dst_ref=lands[side].at[slot, at],
            send_sem=sems[0].at[slot, lane[side], at],
            recv_sem=sems[1].at[slot, lane[side], at],
            device_id=dev[side],
            device_id_type=MESH,
        )

    def sides_of(k, r):
        found = ["lo" if k == 0 else "hi"]
        if r == 0:
            found.append("prev")
        if r == rc - 1:
            found.append("next")
        return found

    def send(slot, k, r):
        for side in sides_of(k, r):
            @pl.when(has[side])
            def _():
                copy(side, slot, k, r).start()

    opposite = {"lo": "hi", "hi": "lo", "prev": "next", "next": "prev"}

    def receive(slot, k, r):
        for side in sides_of(k, r):
            @pl.when(has[side])
            def _():
                copy(opposite[side], slot, k, r).wait_recv()

    base = ka - m
    odd = rad % 2
    nrot = wave.shape[3]

    def give(which, part):
        dest = base + 2 * part + y
        source = (cur_ref, prev_ref, leg_ref)[which]
        if which < 2:
            source = source.at[pl.ds(((part + odd) % 2) * rc, rc)]
            target = wave.at[which, c]
        else:
            target = legs.at[c]
        remote = pltpu.make_async_remote_copy(
            src_ref=source, dst_ref=target,
            send_sem=in_send.at[which, part], recv_sem=in_recv.at[which, c],
            device_id=(dest, rad), device_id_type=MESH,
        )
        return dest, source, target, remote

    def give_start(which):
        for part in range(2):
            dest, source, target, remote = give(which, part)

            @pl.when(dest != ka)
            def _():
                remote.start()

            @pl.when(dest == ka)
            def _():
                target[...] = source[...]

    def give_sent(which):
        for part in range(2):
            dest, _, _, remote = give(which, part)

            @pl.when(dest != ka)
            def _():
                remote.wait_send()

    def take(which):
        for k in range(2):
            @pl.when(base + 2 * c + k != ka)
            def _():
                target = legs.at[k] if which == 2 else wave.at[which, k]
                pltpu.make_async_remote_copy(
                    src_ref=target, dst_ref=target,
                    send_sem=in_send.at[which, 0], recv_sem=in_recv.at[which, k],
                    device_id=(other, rad), device_id_type=MESH,
                ).wait_recv()

    def back_old(slot, k):
        dest = base + 2 * c + k
        return dest, pltpu.make_async_remote_copy(
            src_ref=wave.at[slot, k], dst_ref=prev_out.at[pl.ds(flip * rc, rc)],
            send_sem=old_send.at[k], recv_sem=old_recv.at[y],
            device_id=(dest, rad), device_id_type=MESH,
        )

    def back_new(slot, k, r):
        dest = base + 2 * c + k
        return dest, pltpu.make_async_remote_copy(
            src_ref=wave.at[slot, k, r], dst_ref=cur_out.at[flip * rc + r],
            send_sem=new_send.at[k, r], recv_sem=new_recv.at[y, r],
            device_id=(dest, rad), device_id_type=MESH,
        )

    order = []
    for i in range(rc // 2):
        order.append((i, rc - 1 - i))

    for side, buf in (("lo", from_lo), ("hi", from_hi), ("prev", from_prev), ("next", from_next)):
        @pl.when(jnp.logical_not(has[side]))
        def _():
            buf[...] = jnp.zeros_like(buf)

    barrier = pltpu.get_barrier_semaphore()
    for side in dev:
        @pl.when(has[side])
        def _():
            pl.semaphore_signal(barrier, inc=1, device_id=dev[side], device_id_type=MESH)
    for away in range(1, 4):
        pl.semaphore_signal(
            barrier, inc=1, device_id=(base + (m + away) % 4, rad), device_id_type=MESH
        )
    pl.semaphore_wait(barrier, 3 + sum(has[side].astype(jnp.int32) for side in dev))

    give_start(0)
    give_start(2)
    take(0)
    for rs in order:
        for r in rs:
            for k in range(2):
                send(0, k, r)
    give_start(1)
    take(2)
    for k in range(2):
        leg = legs[k, :nrot]
        top, low = split(leg)
        lb_ref[k] = jnp.concatenate([top, low, top], axis=1)
        top, low = split(leg.T)
        la_ref[k] = jnp.concatenate([top, low, top], axis=1)
        first = legs[k, nrot : nrot + 1, : wave.shape[4]]
        at_row = lax.broadcasted_iota(jnp.int32, wave.shape[3:], 0).astype(jnp.float32)
        live = (at_row >= first).astype(jnp.float32)
        shi_ref[k] = live * here_ref[k]
        slo_ref[k] = live * below_ref[k]
    take(1)

    def step(n, last):
        s = lax.rem(n, 2)
        t = 1 - s
        for i, rs in enumerate(order):
            for k in range(2):
                both = jnp.concatenate([wave[s, k, rs[0]], wave[s, k, rs[1]]], axis=1)
                top, low = split(both)
                ang = jnp.dot(
                    la_ref[k], jnp.concatenate([top, top, low], axis=0),
                    preferred_element_type=jnp.float32,
                )
                ptop, plow = split(ang * pot_ref[i])
                back = jnp.dot(
                    lb_ref[k], jnp.concatenate([ptop, ptop, plow], axis=0),
                    preferred_element_type=jnp.float32,
                )
                width = both.shape[1] // 2
                for e, r in enumerate(rs):
                    cols = slice(e * width, (e + 1) * width)
                    kin = jnp.dot(
                        jnp.concatenate([top[:, cols], low[:, cols]], axis=1), table_ref[...],
                        preferred_element_type=jnp.float32,
                    )
                    kin = kin[:, :width] + kin[:, width:]
                    wave[t, k, r] = (
                        diag_ref[k, r] * wave[s, k, r]
                        + scal_ref[0, r] * kin
                        + back[:, cols]
                        - scal_ref[1, r] * wave[t, k, r]
                    )
            for r in rs:
                for k in range(2):
                    receive(s, k, r)
                    ahead = wave[s, k, r + 1] if r < rc - 1 else from_next[s, k]
                    behind = wave[s, k, r - 1] if r > 0 else from_prev[s, k]
                    upper = wave[s, 1, r] if k == 0 else from_hi[s, r]
                    lower = from_lo[s, r] if k == 0 else wave[s, 0, r]
                    wave[t, k, r] = (
                        wave[t, k, r]
                        - scal_ref[2, r] * (ahead + behind)
                        + scal_ref[3, r] * (shi_ref[k] * upper + slo_ref[k] * lower)
                    )
                    if not last:
                        send(t, k, r)
                    else:
                        dest, remote = back_new(t, k, r)

                        @pl.when(dest != ka)
                        def _():
                            remote.start()

                        @pl.when(dest == ka)
                        def _():
                            cur_out[flip * rc + r] = wave[t, k, r]
        for rs in order:
            for r in rs:
                for k in range(2):
                    for side in sides_of(k, r):
                        @pl.when(has[side])
                        def _():
                            copy(side, s, k, r).wait_send()

    def body(n, carry):
        step(n, False)
        return carry

    lax.fori_loop(0, steps - 1, body, 0)
    slot = (steps - 1) % 2
    for k in range(2):
        dest, remote = back_old(slot, k)

        @pl.when(dest != ka)
        def _():
            remote.start()

        @pl.when(dest == ka)
        def _():
            prev_out[pl.ds(flip * rc, rc)] = wave[slot, k]
    step(steps - 1, True)
    for which in range(3):
        give_sent(which)
    for k in range(2):
        dest, remote = back_old(slot, k)

        @pl.when(dest != ka)
        def _():
            remote.wait_send()
            for r in range(rc):
                back_new(1 - slot, k, r)[1].wait_send()
    for part in range(2):
        at = ((part + odd) % 2) * rc

        @pl.when(base + 2 * part + y != ka)
        def _():
            pltpu.make_async_remote_copy(
                src_ref=wave.at[slot, 0], dst_ref=prev_out.at[pl.ds(at, rc)],
                send_sem=old_send.at[0], recv_sem=old_recv.at[part],
                device_id=(other, rad), device_id_type=MESH,
            ).wait_recv()
            for r in range(rc):
                pltpu.make_async_remote_copy(
                    src_ref=wave.at[1 - slot, 0, r], dst_ref=cur_out.at[at + r],
                    send_sem=new_send.at[0, r], recv_sem=new_recv.at[part, r],
                    device_id=(other, rad), device_id_type=MESH,
                ).wait_recv()


def on_device(prev_wave, cur_wave, legendre, potential, radial, rot_const, first_row):
    nka, nrad = lax.axis_size("ka"), lax.axis_size("rad")
    ka, rad = lax.axis_index("ka"), lax.axis_index("rad")
    nrot, rows, width = cur_wave.shape[1:]
    rc = rows // 2
    m = ka % 4
    hi_bit, lo_bit = m // 2, m % 2
    group = ka // 4
    odd = rad % 2
    jtop = nka - 1
    jidx = jnp.arange(nrot, dtype=jnp.int32)
    mine = (jidx >= first_row[0]).astype(jnp.float32)
    cur = jnp.transpose(cur_wave[0] * mine[:, None, None], (1, 0, 2))
    prev = jnp.transpose(prev_wave[0] * mine[:, None, None], (1, 0, 2))
    packed = jnp.concatenate(
        [legendre[0] * mine[:, None], jnp.broadcast_to(first_row[0].astype(jnp.float32), (8, nrot))]
    )

    half = hi_bit ^ odd
    local = lax.dynamic_slice_in_dim(radial, half * rc, rc, 1)
    damp = jnp.exp(-local[2])
    scal = jnp.stack([damp, damp * damp, 2.0 * COEF * damp, 2.0 * local[1] * damp])
    kval = 4 * group + 2 * lo_bit + jnp.arange(2, dtype=jnp.int32)
    qrot = (jidx * (jidx + 1)).astype(jnp.float32) / (nrot * (nrot + 1))
    pkay = (jtop * (jtop + 1) - 2 * kval * kval).astype(jnp.float32) / (nrot * (nrot + 1))
    diag = (
        rot_const[None, None, None, :] * qrot[None, None, :, None]
        + local[0][None, :, None, None] * (qrot[None, None, :, None] + pkay[:, None, None, None])
        - EMID
    )
    diag = 2.0 * damp[None, :, None, None] * (diag + 2.0 * COEF)
    s_here = coupling(jidx[None, :], kval[:, None], jtop, nrot)
    s_below = coupling(jidx[None, :], kval[:, None] - 1, jtop, nrot)
    s_here = jnp.broadcast_to(s_here[:, :, None], (2, nrot, width))
    s_below = jnp.broadcast_to(s_below[:, :, None], (2, nrot, width))

    top, low = halves(2.0 * sinc_table(width))
    row = jnp.concatenate([top, low], axis=1)
    table = jnp.concatenate([row, row], axis=0)
    pot = lax.dynamic_slice_in_dim(jnp.transpose(potential, (1, 0, 2)), half * rc, rc, 0)
    pot = pot * (2.0 * damp)[:, None, None]
    pot = jnp.stack([jnp.concatenate([pot[i], pot[rc - 1 - i]], axis=1) for i in range(rc // 2)])

    steps = STEPS * KICKS
    vmem = pl.BlockSpec(memory_space=pltpu.VMEM)
    point = (nrot, width)
    whole = jax.ShapeDtypeStruct((rows,) + point, jnp.float32)
    sem = pltpu.SemaphoreType.DMA
    prev_out, cur_out = pl.pallas_call(
        functools.partial(kernel, nka, nrad, steps, rc),
        out_shape=(whole, whole),
        in_specs=[vmem] * 8 + [pl.BlockSpec(memory_space=pltpu.SMEM)],
        out_specs=(vmem, vmem),
        scratch_shapes=[
            pltpu.VMEM((2, 2, rc) + point, jnp.float32),
            pltpu.VMEM((2, nrot + 8, nrot), jnp.float32),
            pltpu.VMEM((2, nrot, 3 * nrot), jnp.bfloat16),
            pltpu.VMEM((2, nrot, 3 * nrot), jnp.bfloat16),
            pltpu.VMEM((2,) + point, jnp.float32),
            pltpu.VMEM((2,) + point, jnp.float32),
            pltpu.VMEM((2, rc) + point, jnp.float32),
            pltpu.VMEM((2, rc) + point, jnp.float32),
            pltpu.VMEM((2, 2) + point, jnp.float32),
            pltpu.VMEM((2, 2) + point, jnp.float32),
            sem((2, 2, rc)), sem((2, 2, rc)), sem((2, 2, 2)), sem((2, 2, 2)),
            sem((3, 2)), sem((3, 2)), sem((2,)), sem((2,)), sem((2, rc)), sem((2, rc)),
        ],
        compiler_params=pltpu.CompilerParams(
            collective_id=0, has_side_effects=True, vmem_limit_bytes=40 * 1024 * 1024
        ),
    )(cur, prev, packed, table, pot, diag, s_here, s_below, scal)
    return (jnp.transpose(prev_out, (1, 0, 2))[None], jnp.transpose(cur_out, (1, 0, 2))[None])


def solution(mesh):
    placed = (
        P("ka", None, "rad", None),
        P("ka", None, "rad", None),
        P("ka", None, None),
        P(None, "rad", None),
        P(None, "rad"),
        P(),
        P("ka"),
    )
    return jax.shard_map(
        on_device,
        mesh=mesh,
        in_specs=placed,
        out_specs=(P("ka", None, "rad", None), P("ka", None, "rad", None)),
        check_vma=False,
    )
```

```python
import functools
import math

import jax
import jax.numpy as jnp
from jax import lax
from jax.experimental import pallas as pl
from jax.experimental.pallas import tpu as pltpu
from jax.sharding import PartitionSpec as P

STEPS = 4
KICKS = 2
COEF = 0.1
RKIN = 0.04
EMID = 0.75
MESH = pl.DeviceIdType.MESH


def sinc_table(count):
    index = jnp.arange(count, dtype=jnp.int32)
    differ = index[:, None] - index[None, :]
    parity = (1 - 2 * (jnp.abs(differ) % 2)).astype(jnp.float32)
    square = jnp.maximum(differ * differ, 1).astype(jnp.float32)
    table = jnp.where(differ == 0, jnp.float32(math.pi * math.pi / 3.0), 2.0 * parity / square)
    return RKIN * table


def coupling(jidx, kval, jtop, nrot):
    first = jnp.maximum(jidx * (jidx + 1) - kval * (kval + 1), 0)
    second = jnp.maximum(jtop * (jtop + 1) - kval * (kval + 1), 0)
    return jnp.sqrt((first * second).astype(jnp.float32)) / (nrot * (jtop + 1))


def halves(x):
    top = lax.reduce_precision(x, 8, 7)
    return top.astype(jnp.bfloat16), (x - top).astype(jnp.bfloat16)


def split(x):
    top = x.astype(jnp.bfloat16)
    return top, (x - top.astype(jnp.float32)).astype(jnp.bfloat16)


def kernel(
    nka, nrad, steps, rc,
    cur_ref, prev_ref, leg_ref, table_ref, pot_ref, diag_ref, here_ref, below_ref, scal_ref,
    prev_out, cur_out,
    wave, legs, la_ref, lb_ref, shi_ref, slo_ref,
    from_lo, from_hi, from_prev, from_next,
    k_send, k_recv, r_send, r_recv, in_send, in_recv, old_in_send, old_in_recv, old_send, old_recv, new_send, new_recv,
):
    ka, rad = lax.axis_index("ka"), lax.axis_index("rad")
    m = ka % 4
    y, c = m // 2, m % 2
    pair = (ka // 4) * 2 + c
    flip = (y + rad) % 2
    chunk = 2 * rad + flip
    has = {
        "lo": pair > 0,
        "hi": pair < nka // 2 - 1,
        "prev": chunk > 0,
        "next": chunk < 2 * nrad - 1,
    }
    other = ka + 2 - 4 * y
    dev = {
        "lo": (jnp.maximum(jnp.where(c == 1, ka - 1, ka - 3), 0), rad),
        "hi": (jnp.minimum(jnp.where(c == 0, ka + 1, ka + 3), nka - 1), rad),
        "prev": (jnp.where(flip == 1, other, ka), jnp.where(flip == 1, rad, jnp.maximum(rad - 1, 0))),
        "next": (jnp.where(flip == 0, other, ka), jnp.where(flip == 0, rad, jnp.minimum(rad + 1, nrad - 1))),
    }
    lands = {"lo": from_hi, "hi": from_lo, "prev": from_next, "next": from_prev}
    lane = {"lo": 0, "hi": 1, "prev": 0, "next": 1}

    def copy(side, slot, k, r):
        if side in ("lo", "hi"):
            sems, at = (k_send, k_recv), r
        else:
            sems, at = (r_send, r_recv), k
        return pltpu.make_async_remote_copy(
            src_ref=wave.at[slot, k, r],
            dst_ref=lands[side].at[slot, at],
            send_sem=sems[0].at[slot, lane[side], at],
            recv_sem=sems[1].at[slot, lane[side], at],
            device_id=dev[side],
            device_id_type=MESH,
        )

    def sides_of(k, r):
        found = []
        if r == 0:
            found.append("prev")
        if r == rc - 1:
            found.append("next")
        return found + ["lo" if k == 0 else "hi"]

    def send(slot, k, r):
        for side in sides_of(k, r):
            @pl.when(has[side])
            def _():
                copy(side, slot, k, r).start()

    opposite = {"lo": "hi", "hi": "lo", "prev": "next", "next": "prev"}

    def receive(slot, k, r):
        for side in sides_of(k, r):
            @pl.when(has[side])
            def _():
                copy(opposite[side], slot, k, r).wait_recv()

    base = ka - m
    odd = rad % 2
    nrot = wave.shape[3]

    def give(which, part):
        dest = base + 2 * part + y
        source = leg_ref
        if which == 0:
            source = cur_ref.at[pl.ds(((part + odd) % 2) * rc, rc)]
            target = wave.at[0, c]
        else:
            target = legs.at[c]
        remote = pltpu.make_async_remote_copy(
            src_ref=source, dst_ref=target,
            send_sem=in_send.at[which, part], recv_sem=in_recv.at[which, c],
            device_id=(dest, rad), device_id_type=MESH,
        )
        return dest, source, target, remote

    def give_prev(part, r):
        dest = base + 2 * part + y
        source = prev_ref.at[((part + odd) % 2) * rc + r]
        target = wave.at[1, c, r]
        remote = pltpu.make_async_remote_copy(
            src_ref=source, dst_ref=target,
            send_sem=old_in_send.at[part, r], recv_sem=old_in_recv.at[c, r],
            device_id=(dest, rad), device_id_type=MESH,
        )
        return dest, source, target, remote

    def take_prev(k, r):
        @pl.when(base + 2 * c + k != ka)
        def _():
            pltpu.make_async_remote_copy(
                src_ref=wave.at[1, k, r], dst_ref=wave.at[1, k, r],
                send_sem=old_in_send.at[0, r], recv_sem=old_in_recv.at[k, r],
                device_id=(other, rad), device_id_type=MESH,
            ).wait_recv()

    def give_start(which):
        for part in range(2):
            dest, source, target, remote = give(which, part)

            @pl.when(dest != ka)
            def _():
                remote.start()

            @pl.when(dest == ka)
            def _():
                target[...] = source[...]

    def give_sent(which):
        for part in range(2):
            dest, _, _, remote = give(which, part)

            @pl.when(dest != ka)
            def _():
                remote.wait_send()

    def take(which):
        for k in range(2):
            @pl.when(base + 2 * c + k != ka)
            def _():
                target = legs.at[k] if which == 2 else wave.at[which, k]
                pltpu.make_async_remote_copy(
                    src_ref=target, dst_ref=target,
                    send_sem=in_send.at[which, 0], recv_sem=in_recv.at[which, k],
                    device_id=(other, rad), device_id_type=MESH,
                ).wait_recv()

    def back_old(slot, k):
        dest = base + 2 * c + k
        return dest, pltpu.make_async_remote_copy(
            src_ref=wave.at[slot, k], dst_ref=prev_out.at[pl.ds(flip * rc, rc)],
            send_sem=old_send.at[k], recv_sem=old_recv.at[y],
            device_id=(dest, rad), device_id_type=MESH,
        )

    def back_new(slot, k, r):
        dest = base + 2 * c + k
        return dest, pltpu.make_async_remote_copy(
            src_ref=wave.at[slot, k, r], dst_ref=cur_out.at[flip * rc + r],
            send_sem=new_send.at[k, r], recv_sem=new_recv.at[y, r],
            device_id=(dest, rad), device_id_type=MESH,
        )

    order = []
    for i in range(rc // 2):
        order.append((i, rc - 1 - i))

    for side, buf in (("lo", from_lo), ("hi", from_hi), ("prev", from_prev), ("next", from_next)):
        @pl.when(jnp.logical_not(has[side]))
        def _():
            buf[...] = jnp.zeros_like(buf)

    barrier = pltpu.get_barrier_semaphore()
    for side in dev:
        @pl.when(has[side])
        def _():
            pl.semaphore_signal(barrier, inc=1, device_id=dev[side], device_id_type=MESH)
    for away in range(1, 4):
        pl.semaphore_signal(
            barrier, inc=1, device_id=(base + (m + away) % 4, rad), device_id_type=MESH
        )
    pl.semaphore_wait(barrier, 3 + sum(has[side].astype(jnp.int32) for side in dev))

    give_start(0)
    give_start(2)
    take(0)
    for rs in order:
        for k in range(2):
            for r in rs:
                send(0, k, r)
    for rs in order:
        for r in rs:
            for part in range(2):
                dest, source, target, remote = give_prev(part, r)

                @pl.when(dest != ka)
                def _():
                    remote.start()

                @pl.when(dest == ka)
                def _():
                    target[...] = source[...]
    take(2)
    for k in range(2):
        leg = legs[k, :nrot]
        top, low = split(leg)
        lb_ref[k] = jnp.concatenate([top, low, top], axis=1)
        top, low = split(leg.T)
        la_ref[k] = jnp.concatenate([top, low, top], axis=1)
        first = legs[k, nrot : nrot + 1, : wave.shape[4]]
        at_row = lax.broadcasted_iota(jnp.int32, wave.shape[3:], 0).astype(jnp.float32)
        live = (at_row >= first).astype(jnp.float32)
        shi_ref[k] = live * here_ref[k]
        slo_ref[k] = live * below_ref[k]
    def step(n, last, first=False):
        s = lax.rem(n, 2)
        t = 1 - s
        for i, rs in enumerate(order):
            for k in range(2):
                both = jnp.concatenate([wave[s, k, rs[0]], wave[s, k, rs[1]]], axis=1)
                top, low = split(both)
                ang = jnp.dot(
                    la_ref[k], jnp.concatenate([top, top, low], axis=0),
                    preferred_element_type=jnp.float32,
                )
                ptop, plow = split(ang * pot_ref[i])
                back = jnp.dot(
                    lb_ref[k], jnp.concatenate([ptop, ptop, plow], axis=0),
                    preferred_element_type=jnp.float32,
                )
                width = both.shape[1] // 2
                for e, r in enumerate(rs):
                    cols = slice(e * width, (e + 1) * width)
                    kin = jnp.dot(
                        jnp.concatenate([top[:, cols], low[:, cols]], axis=1), table_ref[...],
                        preferred_element_type=jnp.float32,
                    )
                    kin = kin[:, :width] + kin[:, width:]
                    if first:
                        take_prev(k, r)
                    wave[t, k, r] = (
                        diag_ref[k, r] * wave[s, k, r]
                        + scal_ref[0, r] * kin
                        + back[:, cols]
                        - scal_ref[1, r] * wave[t, k, r]
                    )
            for k in range(2):
                for r in rs:
                    receive(s, k, r)
                    ahead = wave[s, k, r + 1] if r < rc - 1 else from_next[s, k]
                    behind = wave[s, k, r - 1] if r > 0 else from_prev[s, k]
                    upper = wave[s, 1, r] if k == 0 else from_hi[s, r]
                    lower = from_lo[s, r] if k == 0 else wave[s, 0, r]
                    wave[t, k, r] = (
                        wave[t, k, r]
                        - scal_ref[2, r] * (ahead + behind)
                        + scal_ref[3, r] * (shi_ref[k] * upper + slo_ref[k] * lower)
                    )
                    if not last:
                        send(t, k, r)
                    else:
                        dest, remote = back_new(t, k, r)

                        @pl.when(dest != ka)
                        def _():
                            remote.start()

                        @pl.when(dest == ka)
                        def _():
                            cur_out[flip * rc + r] = wave[t, k, r]
        for rs in order:
            for r in rs:
                for k in range(2):
                    for side in sides_of(k, r):
                        @pl.when(has[side])
                        def _():
                            copy(side, s, k, r).wait_send()

    def body(n, carry):
        step(n, False)
        return carry

    step(0, False, True)
    lax.fori_loop(1, steps - 1, body, 0)
    slot = (steps - 1) % 2
    for k in range(2):
        dest, remote = back_old(slot, k)

        @pl.when(dest != ka)
        def _():
            remote.start()

        @pl.when(dest == ka)
        def _():
            prev_out[pl.ds(flip * rc, rc)] = wave[slot, k]
    step(steps - 1, True)
    for which in (0, 2):
        give_sent(which)
    for part in range(2):
        for r in range(rc):
            dest, _, _, remote = give_prev(part, r)

            @pl.when(dest != ka)
            def _():
                remote.wait_send()
    for k in range(2):
        dest, remote = back_old(slot, k)

        @pl.when(dest != ka)
        def _():
            remote.wait_send()
            for r in range(rc):
                back_new(1 - slot, k, r)[1].wait_send()
    for part in range(2):
        at = ((part + odd) % 2) * rc

        @pl.when(base + 2 * part + y != ka)
        def _():
            pltpu.make_async_remote_copy(
                src_ref=wave.at[slot, 0], dst_ref=prev_out.at[pl.ds(at, rc)],
                send_sem=old_send.at[0], recv_sem=old_recv.at[part],
                device_id=(other, rad), device_id_type=MESH,
            ).wait_recv()
            for r in range(rc):
                pltpu.make_async_remote_copy(
                    src_ref=wave.at[1 - slot, 0, r], dst_ref=cur_out.at[at + r],
                    send_sem=new_send.at[0, r], recv_sem=new_recv.at[part, r],
                    device_id=(other, rad), device_id_type=MESH,
                ).wait_recv()


def on_device(prev_wave, cur_wave, legendre, potential, radial, rot_const, first_row):
    nka, nrad = lax.axis_size("ka"), lax.axis_size("rad")
    ka, rad = lax.axis_index("ka"), lax.axis_index("rad")
    nrot, rows, width = cur_wave.shape[1:]
    rc = rows // 2
    m = ka % 4
    hi_bit, lo_bit = m // 2, m % 2
    group = ka // 4
    odd = rad % 2
    jtop = nka - 1
    jidx = jnp.arange(nrot, dtype=jnp.int32)
    mine = (jidx >= first_row[0]).astype(jnp.float32)
    cur = jnp.transpose(cur_wave[0] * mine[:, None, None], (1, 0, 2))
    prev = jnp.transpose(prev_wave[0] * mine[:, None, None], (1, 0, 2))
    packed = jnp.concatenate(
        [legendre[0] * mine[:, None], jnp.broadcast_to(first_row[0].astype(jnp.float32), (8, nrot))]
    )

    half = hi_bit ^ odd
    local = lax.dynamic_slice_in_dim(radial, half * rc, rc, 1)
    damp = jnp.exp(-local[2])
    scal = jnp.stack([damp, damp * damp, 2.0 * COEF * damp, 2.0 * local[1] * damp])
    kval = 4 * group + 2 * lo_bit + jnp.arange(2, dtype=jnp.int32)
    qrot = (jidx * (jidx + 1)).astype(jnp.float32) / (nrot * (nrot + 1))
    pkay = (jtop * (jtop + 1) - 2 * kval * kval).astype(jnp.float32) / (nrot * (nrot + 1))
    diag = (
        rot_const[None, None, None, :] * qrot[None, None, :, None]
        + local[0][None, :, None, None] * (qrot[None, None, :, None] + pkay[:, None, None, None])
        - EMID
    )
    diag = 2.0 * damp[None, :, None, None] * (diag + 2.0 * COEF)
    s_here = coupling(jidx[None, :], kval[:, None], jtop, nrot)
    s_below = coupling(jidx[None, :], kval[:, None] - 1, jtop, nrot)
    s_here = jnp.broadcast_to(s_here[:, :, None], (2, nrot, width))
    s_below = jnp.broadcast_to(s_below[:, :, None], (2, nrot, width))

    top, low = halves(2.0 * sinc_table(width))
    row = jnp.concatenate([top, low], axis=1)
    table = jnp.concatenate([row, row], axis=0)
    pot = lax.dynamic_slice_in_dim(jnp.transpose(potential, (1, 0, 2)), half * rc, rc, 0)
    pot = pot * (2.0 * damp)[:, None, None]
    pot = jnp.stack([jnp.concatenate([pot[i], pot[rc - 1 - i]], axis=1) for i in range(rc // 2)])

    steps = STEPS * KICKS
    vmem = pl.BlockSpec(memory_space=pltpu.VMEM)
    point = (nrot, width)
    whole = jax.ShapeDtypeStruct((rows,) + point, jnp.float32)
    sem = pltpu.SemaphoreType.DMA
    prev_out, cur_out = pl.pallas_call(
        functools.partial(kernel, nka, nrad, steps, rc),
        out_shape=(whole, whole),
        in_specs=[vmem] * 8 + [pl.BlockSpec(memory_space=pltpu.SMEM)],
        out_specs=(vmem, vmem),
        scratch_shapes=[
            pltpu.VMEM((2, 2, rc) + point, jnp.float32),
            pltpu.VMEM((2, nrot + 8, nrot), jnp.float32),
            pltpu.VMEM((2, nrot, 3 * nrot), jnp.bfloat16),
            pltpu.VMEM((2, nrot, 3 * nrot), jnp.bfloat16),
            pltpu.VMEM((2,) + point, jnp.float32),
            pltpu.VMEM((2,) + point, jnp.float32),
            pltpu.VMEM((2, rc) + point, jnp.float32),
            pltpu.VMEM((2, rc) + point, jnp.float32),
            pltpu.VMEM((2, 2) + point, jnp.float32),
            pltpu.VMEM((2, 2) + point, jnp.float32),
            sem((2, 2, rc)), sem((2, 2, rc)), sem((2, 2, 2)), sem((2, 2, 2)),
            sem((3, 2)), sem((3, 2)), sem((2, rc)), sem((2, rc)), sem((2,)), sem((2,)), sem((2, rc)), sem((2, rc)),
        ],
        compiler_params=pltpu.CompilerParams(
            collective_id=0, has_side_effects=True, vmem_limit_bytes=40 * 1024 * 1024
        ),
    )(cur, prev, packed, table, pot, diag, s_here, s_below, scal)
    return (jnp.transpose(prev_out, (1, 0, 2))[None], jnp.transpose(cur_out, (1, 0, 2))[None])


def solution(mesh):
    placed = (
        P("ka", None, "rad", None),
        P("ka", None, "rad", None),
        P("ka", None, None),
        P(None, "rad", None),
        P(None, "rad"),
        P(),
        P("ka"),
    )
    return jax.shard_map(
        on_device,
        mesh=mesh,
        in_specs=placed,
        out_specs=(P("ka", None, "rad", None), P("ka", None, "rad", None)),
        check_vma=False,
    )
```

```python
import functools
import math

import jax
import jax.numpy as jnp
from jax import lax
from jax.experimental import pallas as pl
from jax.experimental.pallas import tpu as pltpu
from jax.sharding import PartitionSpec as P

STEPS = 4
KICKS = 2
COEF = 0.1
RKIN = 0.04
EMID = 0.75
MESH = pl.DeviceIdType.MESH


def sinc_table(count):
    index = jnp.arange(count, dtype=jnp.int32)
    differ = index[:, None] - index[None, :]
    parity = (1 - 2 * (jnp.abs(differ) % 2)).astype(jnp.float32)
    square = jnp.maximum(differ * differ, 1).astype(jnp.float32)
    table = jnp.where(differ == 0, jnp.float32(math.pi * math.pi / 3.0), 2.0 * parity / square)
    return RKIN * table


def coupling(jidx, kval, jtop, nrot):
    first = jnp.maximum(jidx * (jidx + 1) - kval * (kval + 1), 0)
    second = jnp.maximum(jtop * (jtop + 1) - kval * (kval + 1), 0)
    return jnp.sqrt((first * second).astype(jnp.float32)) / (nrot * (jtop + 1))


def halves(x):
    top = lax.reduce_precision(x, 8, 7)
    return top.astype(jnp.bfloat16), (x - top).astype(jnp.bfloat16)


def split(x):
    top = x.astype(jnp.bfloat16)
    return top, (x - top.astype(jnp.float32)).astype(jnp.bfloat16)


def kernel(
    nka, nrad, steps, rc,
    cur_ref, prev_ref, leg_ref, table_ref, pot_ref, diag_ref, here_ref, below_ref, scal_ref,
    prev_out, cur_out,
    wave, legs, la_ref, lb_ref, shi_ref, slo_ref,
    from_lo, from_hi, from_prev, from_next,
    k_send, k_recv, r_send, r_recv, in_send, in_recv, old_in_send, old_in_recv, edge_send, old_send, old_recv, new_send, new_recv,
):
    ka, rad = lax.axis_index("ka"), lax.axis_index("rad")
    m = ka % 4
    y, c = m // 2, m % 2
    pair = (ka // 4) * 2 + c
    flip = (y + rad) % 2
    chunk = 2 * rad + flip
    has = {
        "lo": pair > 0,
        "hi": pair < nka // 2 - 1,
        "prev": chunk > 0,
        "next": chunk < 2 * nrad - 1,
    }
    other = ka + 2 - 4 * y
    dev = {
        "lo": (jnp.maximum(jnp.where(c == 1, ka - 1, ka - 3), 0), rad),
        "hi": (jnp.minimum(jnp.where(c == 0, ka + 1, ka + 3), nka - 1), rad),
        "prev": (jnp.where(flip == 1, other, ka), jnp.where(flip == 1, rad, jnp.maximum(rad - 1, 0))),
        "next": (jnp.where(flip == 0, other, ka), jnp.where(flip == 0, rad, jnp.minimum(rad + 1, nrad - 1))),
    }
    lands = {"lo": from_hi, "hi": from_lo, "prev": from_next, "next": from_prev}
    lane = {"lo": 0, "hi": 1, "prev": 0, "next": 1}

    def copy(side, slot, k, r):
        if side in ("lo", "hi"):
            sems, at = (k_send, k_recv), r
        else:
            sems, at = (r_send, r_recv), k
        return pltpu.make_async_remote_copy(
            src_ref=wave.at[slot, k, r],
            dst_ref=lands[side].at[slot, at],
            send_sem=sems[0].at[slot, lane[side], at],
            recv_sem=sems[1].at[slot, lane[side], at],
            device_id=dev[side],
            device_id_type=MESH,
        )

    def sides_of(k, r):
        found = []
        if r == 0:
            found.append("prev")
        if r == rc - 1:
            found.append("next")
        return found + ["lo" if k == 0 else "hi"]

    def wanted(side, first, mine):
        if not first or side in ("lo", "hi"):
            return has[side]
        inside = (flip == 1) if side == "prev" else (flip == 0)
        return jnp.logical_and(has[side], jnp.logical_not(jnp.logical_and(inside, mine)))

    def send(slot, k, r, first=False):
        for side in sides_of(k, r):
            @pl.when(wanted(side, first, y != c))
            def _():
                copy(side, slot, k, r).start()

    opposite = {"lo": "hi", "hi": "lo", "prev": "next", "next": "prev"}

    def receive(slot, k, r, first=False):
        for side in sides_of(k, r):
            @pl.when(wanted(side, first, jnp.logical_and(y == c, k == c)))
            def _():
                copy(opposite[side], slot, k, r).wait_recv()

    base = ka - m
    odd = rad % 2
    nrot = wave.shape[3]

    def give(which, part):
        dest = base + 2 * part + y
        source = leg_ref
        if which == 0:
            source = cur_ref.at[pl.ds(((part + odd) % 2) * rc, rc)]
            target = wave.at[0, c]
        else:
            target = legs.at[c]
        remote = pltpu.make_async_remote_copy(
            src_ref=source, dst_ref=target,
            send_sem=in_send.at[which, part], recv_sem=in_recv.at[which, c],
            device_id=(dest, rad), device_id_type=MESH,
        )
        return dest, source, target, remote

    def give_prev(part, r):
        dest = base + 2 * part + y
        source = prev_ref.at[((part + odd) % 2) * rc + r]
        target = wave.at[1, c, r]
        remote = pltpu.make_async_remote_copy(
            src_ref=source, dst_ref=target,
            send_sem=old_in_send.at[part, r], recv_sem=old_in_recv.at[c, r],
            device_id=(dest, rad), device_id_type=MESH,
        )
        return dest, source, target, remote

    def edge(into, row, at):
        return pltpu.make_async_remote_copy(
            src_ref=cur_ref.at[row], dst_ref=into.at[0, c],
            send_sem=edge_send, recv_sem=r_recv.at[0, at, c],
            device_id=(base + 3 * y, rad), device_id_type=MESH,
        )

    def edges(act):
        for value, into, row, at in ((1, from_prev, rc - 1, 1), (0, from_next, rc, 0)):
            @pl.when(jnp.logical_and(flip == value, y != c))
            def _():
                act(edge(into, row, at))

    def take_prev(k, r):
        @pl.when(base + 2 * c + k != ka)
        def _():
            pltpu.make_async_remote_copy(
                src_ref=wave.at[1, k, r], dst_ref=wave.at[1, k, r],
                send_sem=old_in_send.at[0, r], recv_sem=old_in_recv.at[k, r],
                device_id=(other, rad), device_id_type=MESH,
            ).wait_recv()

    def give_start(which):
        for part in range(2):
            dest, source, target, remote = give(which, part)

            @pl.when(dest != ka)
            def _():
                remote.start()

            @pl.when(dest == ka)
            def _():
                target[...] = source[...]

    def give_sent(which):
        for part in range(2):
            dest, _, _, remote = give(which, part)

            @pl.when(dest != ka)
            def _():
                remote.wait_send()

    def take(which):
        for k in range(2):
            @pl.when(base + 2 * c + k != ka)
            def _():
                target = legs.at[k] if which == 2 else wave.at[which, k]
                pltpu.make_async_remote_copy(
                    src_ref=target, dst_ref=target,
                    send_sem=in_send.at[which, 0], recv_sem=in_recv.at[which, k],
                    device_id=(other, rad), device_id_type=MESH,
                ).wait_recv()

    def back_old(slot, k):
        dest = base + 2 * c + k
        return dest, pltpu.make_async_remote_copy(
            src_ref=wave.at[slot, k], dst_ref=prev_out.at[pl.ds(flip * rc, rc)],
            send_sem=old_send.at[k], recv_sem=old_recv.at[y],
            device_id=(dest, rad), device_id_type=MESH,
        )

    def back_new(slot, k, r):
        dest = base + 2 * c + k
        return dest, pltpu.make_async_remote_copy(
            src_ref=wave.at[slot, k, r], dst_ref=cur_out.at[flip * rc + r],
            send_sem=new_send.at[k, r], recv_sem=new_recv.at[y, r],
            device_id=(dest, rad), device_id_type=MESH,
        )

    order = []
    for i in range(rc // 2):
        order.append((i, rc - 1 - i))

    for side, buf in (("lo", from_lo), ("hi", from_hi), ("prev", from_prev), ("next", from_next)):
        @pl.when(jnp.logical_not(has[side]))
        def _():
            buf[...] = jnp.zeros_like(buf)

    barrier = pltpu.get_barrier_semaphore()
    for side in dev:
        @pl.when(has[side])
        def _():
            pl.semaphore_signal(barrier, inc=1, device_id=dev[side], device_id_type=MESH)
    for away in range(1, 4):
        pl.semaphore_signal(
            barrier, inc=1, device_id=(base + (m + away) % 4, rad), device_id_type=MESH
        )
    pl.semaphore_wait(barrier, 3 + sum(has[side].astype(jnp.int32) for side in dev))

    give_start(0)
    edges(lambda remote: remote.start())
    for value, into, row in ((1, from_prev, rc - 1), (0, from_next, rc)):
        @pl.when(jnp.logical_and(flip == value, y == c))
        def _():
            into[0, c] = cur_ref[row]
    give_start(2)
    take(0)
    for rs in order:
        for k in range(2):
            for r in rs:
                send(0, k, r, True)
    for rs in order:
        for r in rs:
            for part in range(2):
                dest, source, target, remote = give_prev(part, r)

                @pl.when(dest != ka)
                def _():
                    remote.start()

                @pl.when(dest == ka)
                def _():
                    target[...] = source[...]
    take(2)
    for k in range(2):
        leg = legs[k, :nrot]
        top, low = split(leg)
        lb_ref[k] = jnp.concatenate([top, low, top], axis=1)
        top, low = split(leg.T)
        la_ref[k] = jnp.concatenate([top, low, top], axis=1)
        first = legs[k, nrot : nrot + 1, : wave.shape[4]]
        at_row = lax.broadcasted_iota(jnp.int32, wave.shape[3:], 0).astype(jnp.float32)
        live = (at_row >= first).astype(jnp.float32)
        shi_ref[k] = live * here_ref[k]
        slo_ref[k] = live * below_ref[k]
    def step(n, last, first=False):
        s = lax.rem(n, 2)
        t = 1 - s
        for i, rs in enumerate(order):
            for k in range(2):
                both = jnp.concatenate([wave[s, k, rs[0]], wave[s, k, rs[1]]], axis=1)
                top, low = split(both)
                ang = jnp.dot(
                    la_ref[k], jnp.concatenate([top, top, low], axis=0),
                    preferred_element_type=jnp.float32,
                )
                ptop, plow = split(ang * pot_ref[i])
                back = jnp.dot(
                    lb_ref[k], jnp.concatenate([ptop, ptop, plow], axis=0),
                    preferred_element_type=jnp.float32,
                )
                width = both.shape[1] // 2
                for e, r in enumerate(rs):
                    cols = slice(e * width, (e + 1) * width)
                    kin = jnp.dot(
                        jnp.concatenate([top[:, cols], low[:, cols]], axis=1), table_ref[...],
                        preferred_element_type=jnp.float32,
                    )
                    kin = kin[:, :width] + kin[:, width:]
                    if first:
                        take_prev(k, r)
                    wave[t, k, r] = (
                        diag_ref[k, r] * wave[s, k, r]
                        + scal_ref[0, r] * kin
                        + back[:, cols]
                        - scal_ref[1, r] * wave[t, k, r]
                    )
            for k in range(2):
                for r in rs:
                    receive(s, k, r, first)
                    ahead = wave[s, k, r + 1] if r < rc - 1 else from_next[s, k]
                    behind = wave[s, k, r - 1] if r > 0 else from_prev[s, k]
                    upper = wave[s, 1, r] if k == 0 else from_hi[s, r]
                    lower = from_lo[s, r] if k == 0 else wave[s, 0, r]
                    wave[t, k, r] = (
                        wave[t, k, r]
                        - scal_ref[2, r] * (ahead + behind)
                        + scal_ref[3, r] * (shi_ref[k] * upper + slo_ref[k] * lower)
                    )
                    if not last:
                        send(t, k, r)
                    else:
                        dest, remote = back_new(t, k, r)

                        @pl.when(dest != ka)
                        def _():
                            remote.start()

                        @pl.when(dest == ka)
                        def _():
                            cur_out[flip * rc + r] = wave[t, k, r]
        for rs in order:
            for r in rs:
                for k in range(2):
                    for side in sides_of(k, r):
                        @pl.when(wanted(side, first, y != c))
                        def _():
                            copy(side, s, k, r).wait_send()

    def body(n, carry):
        step(n, False)
        return carry

    step(0, False, True)
    lax.fori_loop(1, steps - 1, body, 0)
    slot = (steps - 1) % 2
    for k in range(2):
        dest, remote = back_old(slot, k)

        @pl.when(dest != ka)
        def _():
            remote.start()

        @pl.when(dest == ka)
        def _():
            prev_out[pl.ds(flip * rc, rc)] = wave[slot, k]
    step(steps - 1, True)
    edges(lambda remote: remote.wait_send())
    for which in (0, 2):
        give_sent(which)
    for part in range(2):
        for r in range(rc):
            dest, _, _, remote = give_prev(part, r)

            @pl.when(dest != ka)
            def _():
                remote.wait_send()
    for k in range(2):
        dest, remote = back_old(slot, k)

        @pl.when(dest != ka)
        def _():
            remote.wait_send()
            for r in range(rc):
                back_new(1 - slot, k, r)[1].wait_send()
    for part in range(2):
        at = ((part + odd) % 2) * rc

        @pl.when(base + 2 * part + y != ka)
        def _():
            pltpu.make_async_remote_copy(
                src_ref=wave.at[slot, 0], dst_ref=prev_out.at[pl.ds(at, rc)],
                send_sem=old_send.at[0], recv_sem=old_recv.at[part],
                device_id=(other, rad), device_id_type=MESH,
            ).wait_recv()
            for r in range(rc):
                pltpu.make_async_remote_copy(
                    src_ref=wave.at[1 - slot, 0, r], dst_ref=cur_out.at[at + r],
                    send_sem=new_send.at[0, r], recv_sem=new_recv.at[part, r],
                    device_id=(other, rad), device_id_type=MESH,
                ).wait_recv()


def on_device(prev_wave, cur_wave, legendre, potential, radial, rot_const, first_row):
    nka, nrad = lax.axis_size("ka"), lax.axis_size("rad")
    ka, rad = lax.axis_index("ka"), lax.axis_index("rad")
    nrot, rows, width = cur_wave.shape[1:]
    rc = rows // 2
    m = ka % 4
    hi_bit, lo_bit = m // 2, m % 2
    group = ka // 4
    odd = rad % 2
    jtop = nka - 1
    jidx = jnp.arange(nrot, dtype=jnp.int32)
    mine = (jidx >= first_row[0]).astype(jnp.float32)
    cur = jnp.transpose(cur_wave[0] * mine[:, None, None], (1, 0, 2))
    prev = jnp.transpose(prev_wave[0] * mine[:, None, None], (1, 0, 2))
    packed = jnp.concatenate(
        [legendre[0] * mine[:, None], jnp.broadcast_to(first_row[0].astype(jnp.float32), (8, nrot))]
    )

    half = hi_bit ^ odd
    local = lax.dynamic_slice_in_dim(radial, half * rc, rc, 1)
    damp = jnp.exp(-local[2])
    scal = jnp.stack([damp, damp * damp, 2.0 * COEF * damp, 2.0 * local[1] * damp])
    kval = 4 * group + 2 * lo_bit + jnp.arange(2, dtype=jnp.int32)
    qrot = (jidx * (jidx + 1)).astype(jnp.float32) / (nrot * (nrot + 1))
    pkay = (jtop * (jtop + 1) - 2 * kval * kval).astype(jnp.float32) / (nrot * (nrot + 1))
    diag = (
        rot_const[None, None, None, :] * qrot[None, None, :, None]
        + local[0][None, :, None, None] * (qrot[None, None, :, None] + pkay[:, None, None, None])
        - EMID
    )
    diag = 2.0 * damp[None, :, None, None] * (diag + 2.0 * COEF)
    s_here = coupling(jidx[None, :], kval[:, None], jtop, nrot)
    s_below = coupling(jidx[None, :], kval[:, None] - 1, jtop, nrot)
    s_here = jnp.broadcast_to(s_here[:, :, None], (2, nrot, width))
    s_below = jnp.broadcast_to(s_below[:, :, None], (2, nrot, width))

    top, low = halves(2.0 * sinc_table(width))
    row = jnp.concatenate([top, low], axis=1)
    table = jnp.concatenate([row, row], axis=0)
    pot = lax.dynamic_slice_in_dim(jnp.transpose(potential, (1, 0, 2)), half * rc, rc, 0)
    pot = pot * (2.0 * damp)[:, None, None]
    pot = jnp.stack([jnp.concatenate([pot[i], pot[rc - 1 - i]], axis=1) for i in range(rc // 2)])

    steps = STEPS * KICKS
    vmem = pl.BlockSpec(memory_space=pltpu.VMEM)
    point = (nrot, width)
    whole = jax.ShapeDtypeStruct((rows,) + point, jnp.float32)
    sem = pltpu.SemaphoreType.DMA
    prev_out, cur_out = pl.pallas_call(
        functools.partial(kernel, nka, nrad, steps, rc),
        out_shape=(whole, whole),
        in_specs=[vmem] * 8 + [pl.BlockSpec(memory_space=pltpu.SMEM)],
        out_specs=(vmem, vmem),
        scratch_shapes=[
            pltpu.VMEM((2, 2, rc) + point, jnp.float32),
            pltpu.VMEM((2, nrot + 8, nrot), jnp.float32),
            pltpu.VMEM((2, nrot, 3 * nrot), jnp.bfloat16),
            pltpu.VMEM((2, nrot, 3 * nrot), jnp.bfloat16),
            pltpu.VMEM((2,) + point, jnp.float32),
            pltpu.VMEM((2,) + point, jnp.float32),
            pltpu.VMEM((2, rc) + point, jnp.float32),
            pltpu.VMEM((2, rc) + point, jnp.float32),
            pltpu.VMEM((2, 2) + point, jnp.float32),
            pltpu.VMEM((2, 2) + point, jnp.float32),
            sem((2, 2, rc)), sem((2, 2, rc)), sem((2, 2, 2)), sem((2, 2, 2)),
            sem((3, 2)), sem((3, 2)), sem((2, rc)), sem((2, rc)), sem, sem((2,)), sem((2,)), sem((2, rc)), sem((2, rc)),
        ],
        compiler_params=pltpu.CompilerParams(
            collective_id=0, has_side_effects=True, vmem_limit_bytes=40 * 1024 * 1024
        ),
    )(cur, prev, packed, table, pot, diag, s_here, s_below, scal)
    return (jnp.transpose(prev_out, (1, 0, 2))[None], jnp.transpose(cur_out, (1, 0, 2))[None])


def solution(mesh):
    placed = (
        P("ka", None, "rad", None),
        P("ka", None, "rad", None),
        P("ka", None, None),
        P(None, "rad", None),
        P(None, "rad"),
        P(),
        P("ka"),
    )
    return jax.shard_map(
        on_device,
        mesh=mesh,
        in_specs=placed,
        out_specs=(P("ka", None, "rad", None), P("ka", None, "rad", None)),
        check_vma=False,
    )
```
